512 devices in a mesh: row: 32 (over y, z_hi, core), col: 16 (over z_lo, x).
Axes of the slice: x: 4, y: 4, z: 16 (z_hi: 4, z_lo: 4; z = z_hi * 4 + z_lo), core: 2. Of those that a mesh axis runs over, the one named last changes fastest.
Arguments:
- pair: bfloat16 [2048, 2048, 128], P('row', 'col'), may hold values from -6 to 6
- atoms: bfloat16 [32768, 128], P(('row', 'col')), may hold values from -6 to 6
- atom_token: int32 [32768], P(('row', 'col')), may hold values from 0 to 2047, as said below
- atom_mask: int32 [32768], P(('row', 'col')), may hold values from 0 to 1, as said below
- bias_gain: float32 [128], replicated, may hold values from 0.5 to 1.5
- w_pair_bias: bfloat16 [128, 4], replicated, may hold values from -0.75 to 0.75
- trans_gain: float32 [128], replicated, may hold values from 0.5 to 1.5
- w_pair_up: bfloat16 [128, 1024], replicated, may hold values from -0.5 to 0.5
- w_pair_down: bfloat16 [512, 128], replicated, may hold values from -0.25 to 0.25
- atom_gain: float32 [128], replicated, may hold values from 0.5 to 1.5
- w_query: bfloat16 [128, 128], replicated
- w_key: bfloat16 [128, 128], replicated
- w_value: bfloat16 [128, 128], replicated, may hold values from -0.5 to 0.5
- w_gate: bfloat16 [128, 128], replicated, may hold values from -1 to 1
- w_out: bfloat16 [128, 128], replicated, may hold values from -0.75 to 0.75
- mid_gain: float32 [128], replicated, may hold values from 0.5 to 1.5
- w_atom_up: bfloat16 [128, 512], replicated, may hold values from -0.5 to 0.5
- w_atom_down: bfloat16 [256, 128], replicated, may hold values from -0.5 to 0.5
- w_single: bfloat16 [128, 384], replicated, may hold values from -0.5 to 0.5
- w_outer_row: bfloat16 [384, 128], replicated, may hold values from -0.4375 to 0.4375
- w_outer_col: bfloat16 [384, 128], replicated, may hold values from -0.4375 to 0.4375
Outputs:
- atoms_out: bfloat16 [32768, 128], P(('row', 'col'))
- pair_out: bfloat16 [2048, 2048, 128], P('row', 'col')
The draws below stay inside these ranges and needn't reach their ends.
Inputs may be any that keep to these rules, and one draw needn't show every extreme that they name: `atom_token`: the atoms of block j (atoms j * 64 to (j + 1) * 64 - 1) name only tokens j * 4 to (j + 1) * 4 - 1, so no token is shared between blocks; along a block the token numbers never decrease; every token has at least one atom with mask 1. `atom_mask`: within each block of 64 atoms the ones come first, at least 48 of them.
All inputs are finite; a program needn't handle non-finite values.
Results may differ from the reference program's by a relative error of at most 0.0074.
Values may be sent and summed in bfloat16 or wider, within the bound.
No kernel may reach another device: no remote copies, remote signals or barrier semaphores. Data moves between devices by JAX's collectives and lax.ppermute only.
A program may use at most 64 MiB of HBM per device.

```python
import jax
import jax.numpy as jnp
from jax import lax

CA = 128
HA = 4
HD = 32
FA = 256
CP = 128
FP = 512
CS = 384
QW = 32
KW = 128
ATOM_DEV = 64
TOK_ATOM = 4
ATOMS = 32768
TOKENS = 2048


def atom_layout(key):
    devices = ATOMS // ATOM_DEV
    least = ATOM_DEV * 3 // 4
    count_key, cut_key = jax.random.split(jax.random.fold_in(key, 101))
    live = jax.random.randint(count_key, (devices,), least, ATOM_DEV + 1)
    live = live.at[0].set(least).at[devices - 1].set(ATOM_DEV)
    position = jnp.arange(ATOM_DEV, dtype=jnp.int32)

    def one_block(block_key):
        order = jax.random.permutation(block_key, least - 1) + 1
        cuts = jnp.sort(order[:TOK_ATOM - 1])
        return jnp.sum((position[:, None] >= cuts[None, :]).astype(jnp.int32), axis=1)
    local = jax.vmap(one_block)(jax.random.split(cut_key, devices))
    tokens = local + TOK_ATOM * jnp.arange(devices, dtype=jnp.int32)[:, None]
    mask = (position[None, :] < live[:, None]).astype(jnp.int32)
    return (tokens.reshape(-1).astype(jnp.int32), mask.reshape(-1))


def draw_atom_token(key, part):
    return atom_layout(key)[0]


def draw_atom_mask(key, part):
    return atom_layout(key)[1]


def draw_w_query(key, part):
    key = jax.random.fold_in(key, 5)
    fresh = jax.random.normal(key, (CA, CA), jnp.float32) * CA ** (-0.5)
    weight = fresh
    return weight.astype(jnp.bfloat16)


def draw_w_key(key, part):
    key = jax.random.fold_in(key, 7)
    fresh = jax.random.normal(key, (CA, CA), jnp.float32) * CA ** (-0.5)
    weight = fresh
    return weight.astype(jnp.bfloat16)


def shard_levels(own_key, dims, shards, low, high):
    gain, own = 1.0, jax.random.fold_in(own_key, 6)
    for dim, shards_of in shards:
        draws = jnp.exp(jax.random.uniform(jax.random.fold_in(own, dim), (shards_of,), jnp.float32, low / len(shards), high / len(shards)))
        gain = gain * jnp.repeat(draws, dims[dim] // shards_of).reshape([-1 if axis == dim else 1 for axis in range(len(dims))])
    return gain


def gaussian(stream_key, dims, deviation, limit, pieces=(), kind=jnp.bfloat16):
    array = deviation * jax.random.normal(stream_key, dims, jnp.float32)
    if pieces:
        array = array * shard_levels(stream_key, dims, pieces, -0.22, 0.18)
    return jnp.clip(array, -limit, limit).astype(kind)


def setup_inputs(seed: int = 0) -> dict:
    arg_keys = jax.random.split(jax.random.key(seed), 22)
    return {
        "pair": gaussian(arg_keys[0], (TOKENS, TOKENS, CP), 1.0, 6.0, ((0, 32), (1, 16))),
        "atoms": gaussian(arg_keys[1], (ATOMS, CA), 1.0, 6.0, ((0, 512),)),
        "atom_token": draw_atom_token(jax.random.fold_in(arg_keys[21], 71), 0),
        "atom_mask": draw_atom_mask(jax.random.fold_in(arg_keys[21], 71), 0),
        "bias_gain": jnp.clip(jax.random.uniform(arg_keys[4], (CP,), jnp.float32, 0.5, 1.5), 0.5, 1.5),
        "w_pair_bias": gaussian(arg_keys[5], (CP, HA), (CP // 2) ** -0.5, 0.75),
        "trans_gain": jnp.clip(jax.random.uniform(arg_keys[6], (CP,), jnp.float32, 0.5, 1.5), 0.5, 1.5),
        "w_pair_up": gaussian(arg_keys[7], (CP, 2 * FP), CP ** -0.5, 0.5),
        "w_pair_down": gaussian(arg_keys[8], (FP, CP), FP ** -0.5, 0.25),
        "atom_gain": jnp.clip(jax.random.uniform(arg_keys[9], (CA,), jnp.float32, 0.5, 1.5), 0.5, 1.5),
        "w_query": draw_w_query(jax.random.fold_in(arg_keys[21], 71), 0),
        "w_key": draw_w_key(jax.random.fold_in(arg_keys[21], 71), 0),
        "w_value": gaussian(arg_keys[12], (CA, CA), CA ** -0.5, 0.5),
        "w_gate": gaussian(arg_keys[13], (CA, CA), (CA // 4) ** -0.5, 1.0),
        "w_out": gaussian(arg_keys[14], (CA, CA), (CA // 2) ** -0.5, 0.75),
        "mid_gain": jnp.clip(jax.random.uniform(arg_keys[15], (CA,), jnp.float32, 0.5, 1.5), 0.5, 1.5),
        "w_atom_up": gaussian(arg_keys[16], (CA, 2 * FA), CA ** -0.5, 0.5),
        "w_atom_down": gaussian(arg_keys[17], (FA, CA), (FA // 2) ** -0.5, 0.5),
        "w_single": gaussian(arg_keys[18], (CA, CS), CA ** -0.5, 0.5),
        "w_outer_row": gaussian(arg_keys[19], (CS, CP), (CS // 2) ** -0.5, 0.4375),
        "w_outer_col": gaussian(arg_keys[20], (CS, CP), (CS // 2) ** -0.5, 0.4375),
    }


def layer_norm(values):
    mean = lax.optimization_barrier(jnp.mean(values, axis=-1, keepdims=True))
    centred = values - mean
    var = lax.optimization_barrier(jnp.mean(centred * centred, axis=-1, keepdims=True))
    return centred * lax.rsqrt(var + 1e-05)

def reference(pair, atoms, atom_token, atom_mask, bias_gain, w_pair_bias, trans_gain, w_pair_up, w_pair_down, atom_gain, w_query, w_key, w_value, w_gate, w_out, mid_gain, w_atom_up, w_atom_down, w_single, w_outer_row, w_outer_col):
    step = 8
    blocks = pair.reshape(TOKENS // step, step, TOKENS, CP)

    def bias_block(block):
        normed = layer_norm(block.astype(jnp.float32))
        normed_bias = (normed * bias_gain).astype(jnp.bfloat16)
        return jnp.einsum('tuc,ch->htu', normed_bias.astype(jnp.float32), w_pair_bias.astype(jnp.float32)).astype(jnp.bfloat16)
    bias_table = lax.map(bias_block, blocks)
    bias_table = jnp.transpose(bias_table, (1, 0, 2, 3)).reshape(HA, TOKENS, TOKENS)
    atom_norm = (layer_norm(atoms.astype(jnp.float32)) * atom_gain).astype(jnp.bfloat16)
    query = jnp.dot(atom_norm, w_query, preferred_element_type=jnp.float32).astype(jnp.bfloat16)
    key = jnp.dot(atom_norm, w_key, preferred_element_type=jnp.float32).astype(jnp.bfloat16)
    value = jnp.dot(atom_norm, w_value, preferred_element_type=jnp.float32).astype(jnp.bfloat16)
    gate_lin = jnp.dot(atom_norm, w_gate, preferred_element_type=jnp.float32)
    rim = (KW - QW) // 2
    key_pad = jnp.pad(key, ((rim, rim), (0, 0)))
    value_pad = jnp.pad(value, ((rim, rim), (0, 0)))
    token_pad = jnp.pad(atom_token, (rim, rim))
    mask_pad = jnp.pad(atom_mask, (rim, rim))
    windows = ATOMS // QW
    slots = (jnp.arange(windows, dtype=jnp.int32) * QW)[:, None] + jnp.arange(KW, dtype=jnp.int32)[None, :]
    key_win = key_pad[slots].reshape(windows, KW, HA, HD).astype(jnp.float32)
    value_win = value_pad[slots].reshape(windows, KW, HA, HD).astype(jnp.float32)
    query_win = query.reshape(windows, QW, HA, HD).astype(jnp.float32)
    query_tok = atom_token.reshape(windows, QW)
    key_tok = token_pad[slots]
    valid = mask_pad[slots] == 1
    bias = bias_table[:, query_tok[:, :, None], key_tok[:, None, :]].astype(jnp.float32)
    bias = jnp.transpose(bias, (1, 0, 2, 3))
    logits = jnp.einsum('wqhd,wkhd->whqk', query_win, key_win) * (1.0 / HD ** 0.5) + bias
    logits = jnp.where(valid[:, None, None, :], logits, -1000000000.0)
    top = lax.optimization_barrier(jnp.max(logits, axis=-1, keepdims=True))
    expo = jnp.exp(logits - top)
    weights = (expo / lax.optimization_barrier(jnp.sum(expo, axis=-1, keepdims=True))).astype(jnp.bfloat16)
    attended = jnp.einsum('whqk,wkhd->wqhd', weights.astype(jnp.float32), value_win).reshape(ATOMS, CA)
    gated = (attended * jax.nn.sigmoid(gate_lin)).astype(jnp.bfloat16)
    atoms_mid = atoms.astype(jnp.float32) + jnp.dot(gated, w_out, preferred_element_type=jnp.float32)
    mid_norm = (layer_norm(atoms_mid) * mid_gain).astype(jnp.bfloat16)
    gate_up = jnp.dot(mid_norm, w_atom_up, preferred_element_type=jnp.float32)
    atom_hidden = (jax.nn.silu(gate_up[:, :FA]) * gate_up[:, FA:]).astype(jnp.bfloat16)
    atoms_out = (atoms_mid + jnp.dot(atom_hidden, w_atom_down, preferred_element_type=jnp.float32)).astype(jnp.bfloat16)
    single_terms = jax.nn.relu(jnp.dot(atoms_out, w_single, preferred_element_type=jnp.float32))
    live = atom_mask.astype(jnp.float32)
    sums = jax.ops.segment_sum(single_terms * live[:, None], atom_token, num_segments=TOKENS)
    counts = jax.ops.segment_sum(live, atom_token, num_segments=TOKENS)
    singles = (sums / counts[:, None]).astype(jnp.bfloat16)
    row_terms = jnp.dot(singles, w_outer_row, preferred_element_type=jnp.float32).astype(jnp.bfloat16)
    col_terms = jnp.dot(singles, w_outer_col, preferred_element_type=jnp.float32).astype(jnp.bfloat16)

    def pair_block(items):
        block, row_part = items
        normed = layer_norm(block.astype(jnp.float32))
        normed_trans = (normed * trans_gain).astype(jnp.bfloat16)
        pair_gu = jnp.dot(normed_trans.reshape(-1, CP), w_pair_up, preferred_element_type=jnp.float32)
        pair_hidden = (jax.nn.silu(pair_gu[:, :FP]) * pair_gu[:, FP:]).astype(jnp.bfloat16)
        pair_update = jnp.dot(pair_hidden, w_pair_down, preferred_element_type=jnp.float32).reshape(block.shape)
        total = block.astype(jnp.float32) + pair_update + row_part.astype(jnp.float32)[:, None, :] + col_terms.astype(jnp.float32)[None, :, :]
        return total.astype(jnp.bfloat16)
    pair_out = lax.map(pair_block, (blocks, row_terms.reshape(TOKENS // step, step, CP)))
    return (atoms_out, pair_out.reshape(TOKENS, TOKENS, CP))
```

```python
import functools

import jax
import jax.numpy as jnp
from jax import lax
from jax.experimental import pallas as pl
from jax.experimental.pallas import tpu as pltpu
from jax.sharding import PartitionSpec as P

F32 = jnp.float32
BF16 = jnp.bfloat16
N4 = 4
QW = 32
KW = 128
RIM = (KW - QW) // 2
ATOMS = 64
EXT = ATOMS + 2 * RIM
HEADS = 4
HEAD = 32
PACK = 80
FAR = -3.0e38
SPLIT = 40
PAIR_ROWS = 8


def rank(y, zh, core, zl, x):
    return ((y * N4 + zh) * 2 + core) * 16 + zl * N4 + x


Z_GROUPS = [
    [rank(y, zh, core, zl, x) for zh in range(N4) for zl in range(N4)]
    for y in range(N4)
    for core in range(2)
    for x in range(N4)
]
PLANE_GROUPS = [
    [rank(y, zh, core, zl, x) for y in range(N4) for x in range(N4)]
    for zh in range(N4)
    for core in range(2)
    for zl in range(N4)
]
CORE_GROUPS = [[2 * i, 2 * i + 1] for i in range(16)]


def dot(a, b):
    return jnp.dot(a, b, preferred_element_type=F32)


def iota(shape, dim):
    return lax.broadcasted_iota(jnp.int32, shape, dim)


def layer_norm(values):
    mean = jnp.mean(values, axis=-1, keepdims=True)
    centred = values - mean
    var = jnp.mean(centred * centred, axis=-1, keepdims=True)
    return centred * lax.rsqrt(var + 1e-05)


def band_kernel(place, pair, gain, weight, atoms, token, mask, band, pack):
    offset = place[0]
    half = (iota((8, 128), 1) % 32) // 16
    pieces = []
    for k in range(16):
        halves, inside = [], []
        for a in range(2):
            start = offset + 16 * ((k - 1) // 4 + a)
            inside.append((start >= 0) & (start <= 112))
            begin = pl.multiple_of(jnp.clip(start, 0, 112), 16)
            halves.append(pair[4 * k : 4 * k + 4, pl.ds(begin, 16), :])
        block = jnp.concatenate(halves, axis=1).reshape(128, 128).astype(F32)
        normed = (layer_norm(block) * gain[...]).astype(BF16)
        table = lax.dot_general(
            weight[...], normed, (((1,), (1,)), ((), ())), preferred_element_type=F32
        )
        table = jnp.concatenate([table, jnp.zeros_like(table)], axis=0)
        keep = jnp.where(half == 0, inside[0].astype(jnp.int32), inside[1].astype(jnp.int32))
        pieces.append(jnp.where(keep > 0, table, 0.0))
    band[...] = jnp.concatenate(pieces, axis=0).astype(BF16)
    pack[0:64, :] = atoms[...]
    lanes = iota((16, 64), 0)
    local = (token[...] - place[1]).astype(F32)
    live = mask[...].astype(F32)
    rows = jnp.where(lanes == 0, local, jnp.where(lanes == 1, live, 0.0))
    pack[64:80, :] = jnp.concatenate([rows, jnp.zeros_like(rows)], axis=1).astype(BF16)


def logit_kernel(
    place, own, left, right, gain, w_query, w_key, w_value, w_gate,
    logits, state, key_pick, query_pick, value, gate,
):
    ext = jnp.concatenate([left[16:64, :], own[0:64, :], right[0:48, :]], axis=0).astype(F32)
    normed = (layer_norm(ext) * gain[...]).astype(BF16)
    mine = normed[RIM : RIM + ATOMS, :]
    query = dot(mine, w_query[...]).astype(BF16)
    key = dot(normed, w_key[...]).astype(BF16)
    value[...] = dot(normed, w_value[...]).astype(BF16)
    gate[...] = jax.nn.sigmoid(dot(mine, w_gate[...]))
    head_of = iota((ATOMS, 128), 1) // HEAD
    zero = jnp.zeros_like(query)
    wide = jnp.concatenate([jnp.where(head_of == h, query, zero) for h in range(HEADS)], axis=0)
    logits[...] = lax.dot_general(
        wide, key, (((1,), (1,)), ((), ())), preferred_element_type=F32
    ) * (1.0 / HEAD**0.5)
    lane, spot = iota((128, EXT), 0), iota((128, EXT), 1)

    def moved(ref, low, high, shift):
        pick = (lane >= low) & (lane < high) & (lane + shift == spot)
        return dot(ref[64:80, :], pick.astype(F32).astype(BF16))

    facts = (
        moved(left, 16, 64, -16) + moved(own, 0, 64, RIM) + moved(right, 0, 48, RIM + ATOMS)
    )
    where = iota((1, EXT), 1)
    token = facts[0:1, :] + jnp.where(
        where >= RIM + ATOMS, 8.0, jnp.where(where >= RIM, 4.0, 0.0)
    )
    first = (iota((ATOMS, EXT), 0) // QW) * QW
    column = iota((ATOMS, EXT), 1)
    near = (column >= first) & (column < first + KW)
    live = jnp.broadcast_to(facts[1:2, :], (ATOMS, EXT))
    state[...] = jnp.where(near, jnp.where(live > 0.5, 1.0, 0.0), -1.0)
    key_pick[...] = (
        ((lane % 32) == token.astype(jnp.int32) + place[0]).astype(F32).astype(BF16)
    )
    own_row = own[64:80, :].astype(F32)[0:1, :]
    square = iota((ATOMS, 128), 0) == iota((ATOMS, 128), 1)
    own_token = jnp.sum(jnp.where(square, own_row, 0.0), axis=1, keepdims=True)
    query_pick[...] = (iota((ATOMS, 128), 1) // 32 == own_token.astype(jnp.int32)).astype(F32)


def atom_kernel(
    band, logits, state, key_pick, query_pick, value, gate, pack, w_out, mid_gain, w_up, w_down,
    w_single, w_row, w_col, atoms_out, terms,
):
    table = jnp.sum(band[...].astype(F32).reshape(16, 8, 128), axis=0)
    picked = jnp.concatenate([query_pick[...] * table[h : h + 1, :] for h in range(HEADS)], axis=0)
    bias = dot(picked.astype(BF16), key_pick[...])
    states = jnp.concatenate([state[...]] * HEADS, axis=0)
    scores = jnp.where(
        states > 0.5, logits[...] + bias, jnp.where(states > -0.5, -1000000000.0, FAR)
    )
    top = jnp.max(scores, axis=-1, keepdims=True)
    expo = jnp.exp(scores - top)
    weights = (expo / jnp.sum(expo, axis=-1, keepdims=True)).astype(BF16)
    mixed = dot(weights, value[...])
    head_of = iota((ATOMS, 128), 1) // HEAD
    attended = jnp.zeros((ATOMS, 128), F32)
    for h in range(HEADS):
        attended = jnp.where(head_of == h, mixed[h * ATOMS : (h + 1) * ATOMS, :], attended)
    gated = (attended * gate[...]).astype(BF16)
    mid = pack[0:64, :].astype(F32) + dot(gated, w_out[...])
    mid_norm = (layer_norm(mid) * mid_gain[...]).astype(BF16)
    gate_up = dot(mid_norm, w_up[...])
    width = gate_up.shape[1] // 2
    half = 0.5 * gate_up[:, :width]
    hidden = ((half + half * jnp.tanh(half)) * gate_up[:, width:]).astype(BF16)
    out = (mid + dot(hidden, w_down[...])).astype(BF16)
    atoms_out[...] = out
    single = jnp.maximum(dot(out, w_single[...]), 0.0)
    facts = pack[64:80, :].astype(F32)
    chosen = jnp.where(
        (iota((8, 128), 0) % 4).astype(F32) == facts[0:1, :], facts[1:2, :], 0.0
    )[:, 0:64]
    counts = jnp.sum(chosen, axis=-1, keepdims=True)
    chosen = chosen.astype(BF16)
    high = single.astype(BF16)
    low = (single - high.astype(F32)).astype(BF16)
    singles = ((dot(chosen, high) + dot(chosen, low)) / counts).astype(BF16)
    col, row = dot(singles, w_col[...]), dot(singles, w_row[...])
    both = jnp.where(iota((8, 128), 0) < 4, col, row)
    terms[...] = jnp.concatenate([both] * 16, axis=0).astype(BF16)


def spread_kernel(place, came, _after, going):
    tiles = came[...].astype(F32).reshape(16, 8, 128)
    cols, rows = [], jnp.zeros((16, 128), F32)
    for zh in range(N4):
        group = [tiles[zh * N4 + zl] for zl in range(N4)]
        cols.append(jnp.concatenate([t[0:4] for t in group], axis=0))
        mine = jnp.concatenate([t[4:8] for t in group], axis=0)
        rows = jnp.where(place[0] == zh, mine, rows)
    plane = jnp.concatenate([piece for col in cols for piece in (col, rows)], axis=0)
    going[...] = jnp.concatenate([plane] * N4, axis=0).astype(BF16)


def settle_kernel(place, came, _after, cols, rows):
    def ordered(start, low):
        begin = pl.multiple_of(start * 128, 128)
        part = came[pl.ds(begin, 128), :].astype(F32).reshape(N4, 32, 128)
        return jnp.concatenate(
            [
                part[x, low + 4 * zl : low + 4 * zl + 4]
                for zl in range(N4)
                for x in range(N4)
            ],
            axis=0,
        )

    cols[...] = ordered(place[0], 0).astype(BF16)
    rows[...] = ordered(place[1], 16)


def transition_kernel(pair, gain, w_up, w_down, *rest):
    out = rest[-1]
    block = pair[...].reshape(-1, 128).astype(F32)
    normed = (layer_norm(block) * gain[...]).astype(BF16)
    gate_up = dot(normed, w_up[...])
    width = gate_up.shape[1] // 2
    half = 0.5 * gate_up[:, :width]
    hidden = ((half + half * jnp.tanh(half)) * gate_up[:, width:]).astype(BF16)
    total = block + dot(hidden, w_down[...])
    out[...] = total.astype(BF16).reshape(out.shape)


def add_kernel(part, rows, cols, out):
    step = part.shape[0]
    begin = pl.multiple_of(pl.program_id(0) * step, step)
    row = rows[pl.ds(begin, step), :]
    total = part[...].astype(F32) + row[:, None, :] + cols[...].astype(F32)[None, :, :]
    out[...] = total.astype(BF16)


def whole(count):
    return [pl.BlockSpec(memory_space=pltpu.VMEM)] * count


SCALARS = pl.BlockSpec(memory_space=pltpu.SMEM)
PARAMS = pltpu.CompilerParams(vmem_limit_bytes=40 * 1024 * 1024)


def cost(flops, moved, trans=0):
    return pl.CostEstimate(flops=flops, bytes_accessed=moved, transcendentals=trans)


def transition(pair, gain, w_up, w_down, first, last, before=None):
    blocks = (last - first) // PAIR_ROWS
    start = first // PAIR_ROWS
    at = lambda i: (i + start, 0, 0)
    block = pl.BlockSpec((PAIR_ROWS, 128, 128), at)
    fixed = lambda shape: pl.BlockSpec(shape, lambda i: (0, 0))
    specs = [block, fixed((1, 128)), fixed(w_up.shape), fixed(w_down.shape)]
    given = [pair, gain, w_up, w_down]
    if before is not None:
        specs.append(pl.BlockSpec(memory_space=pl.ANY))
        given.append(before)
    count = (last - first) * 128
    return pl.pallas_call(
        transition_kernel,
        grid=(blocks,),
        in_specs=specs,
        out_specs=block,
        out_shape=jax.ShapeDtypeStruct(pair.shape, BF16),
        input_output_aliases={} if before is None else {4: 0},
        compiler_params=PARAMS,
        cost_estimate=cost(count * 4 * 196608, count * 512, count * 512),
    )(*given)


def body(
    pair, atoms, atom_token, atom_mask, bias_gain, w_pair_bias, trans_gain, w_pair_up, w_pair_down,
    atom_gain, w_query, w_key, w_value, w_gate, w_out, mid_gain, w_atom_up, w_atom_down, w_single,
    w_outer_row, w_outer_col,
):
    row, col = lax.axis_index("row"), lax.axis_index("col")
    joint = ("row", "col")
    y, zh, zl = row // 8, (row // 2) % 4, col // 4
    i32 = jnp.int32
    place_band = jnp.stack([64 * row - 128 * col, 4 * (row * 16 + col)]).astype(i32)
    place_shift = (4 * ((col + 3) % 4)).astype(i32)[None]
    place_zh = zh.astype(i32)[None]
    place_end = jnp.stack([zl, y]).astype(i32)
    shape = jax.ShapeDtypeStruct

    band, pack = pl.pallas_call(
        band_kernel,
        in_specs=[SCALARS] + whole(6),
        out_specs=whole(2),
        out_shape=[shape((128, 128), BF16), shape((PACK, 128), BF16)],
        compiler_params=PARAMS,
        cost_estimate=cost(2048 * 2048, 1 << 21),
    )(
        place_band,
        pair,
        bias_gain[None],
        w_pair_bias.T,
        atoms,
        atom_token[None],
        atom_mask[None],
    )
    own_band = lax.all_to_all(band, "col", 0, 0, tiled=True)
    count = 512
    left = lax.ppermute(pack, joint, [(i, i + 1) for i in range(count - 1)])
    right = lax.ppermute(pack, joint, [(i + 1, i) for i in range(count - 1)])
    prepared = pl.pallas_call(
        logit_kernel,
        in_specs=[SCALARS] + whole(8),
        out_specs=whole(6),
        out_shape=[
            shape((HEADS * ATOMS, EXT), F32),
            shape((ATOMS, EXT), F32),
            shape((128, EXT), BF16),
            shape((ATOMS, 128), F32),
            shape((EXT, 128), BF16),
            shape((ATOMS, 128), F32),
        ],
        compiler_params=PARAMS,
        cost_estimate=cost(1 << 24, 1 << 19),
    )(place_shift, pack, left, right, atom_gain[None], w_query, w_key, w_value, w_gate)
    atoms_out, terms = pl.pallas_call(
        atom_kernel,
        in_specs=whole(15),
        out_specs=whole(2),
        out_shape=[shape((ATOMS, 128), BF16), shape((128, 128), BF16)],
        compiler_params=PARAMS,
        cost_estimate=cost(1 << 25, 1 << 20),
    )(
        own_band, *prepared, pack, w_out, mid_gain[None], w_atom_up, w_atom_down, w_single,
        w_outer_row, w_outer_col,
    )
    along = lax.all_to_all(terms, joint, 0, 0, tiled=True, axis_index_groups=Z_GROUPS)
    held, _ = lax.optimization_barrier((trans_gain, terms))
    part = transition(pair, held[None], w_pair_up, w_pair_down, 0, SPLIT)
    hold = pl.BlockSpec(memory_space=pl.ANY)
    going = pl.pallas_call(
        spread_kernel,
        in_specs=[SCALARS] + whole(1) + [hold],
        out_specs=whole(1)[0],
        out_shape=shape((512, 128), BF16),
        compiler_params=PARAMS,
    )(place_zh, along, part)
    came = lax.all_to_all(going, joint, 0, 0, tiled=True, axis_index_groups=PLANE_GROUPS)
    held, _ = lax.optimization_barrier((trans_gain, going))
    part = transition(pair, held[None], w_pair_up, w_pair_down, SPLIT, 64, part)
    cols, rows = pl.pallas_call(
        settle_kernel,
        in_specs=[SCALARS] + whole(1) + [hold],
        out_specs=whole(2),
        out_shape=[shape((64, 128), BF16), shape((64, 128), F32)],
        compiler_params=PARAMS,
    )(place_end, came, part)
    cols = lax.all_gather(cols, "row", axis=0, tiled=True, axis_index_groups=CORE_GROUPS)
    block = pl.BlockSpec((16, 128, 128), lambda i: (i, 0, 0))
    pair_out = pl.pallas_call(
        add_kernel,
        grid=(4,),
        in_specs=[
            block,
            pl.BlockSpec((64, 128), lambda i: (0, 0)),
            pl.BlockSpec((128, 128), lambda i: (0, 0)),
        ],
        out_specs=block,
        out_shape=shape(pair.shape, BF16),
        compiler_params=PARAMS,
    )(part, rows, cols)
    return (atoms_out, pair_out)


def solution(mesh):
    spread = P(("row", "col"))
    in_specs = (P("row", "col", None), P(("row", "col"), None), spread, spread) + (P(),) * 17
    out_specs = (P(("row", "col"), None), P("row", "col", None))
    return jax.shard_map(body, mesh=mesh, in_specs=in_specs, out_specs=out_specs, check_vma=False)
```

```python
import functools

import jax
import jax.numpy as jnp
from jax import lax
from jax.experimental import pallas as pl
from jax.experimental.pallas import tpu as pltpu
from jax.sharding import PartitionSpec as P

F32 = jnp.float32
BF16 = jnp.bfloat16
N4 = 4
QW = 32
KW = 128
RIM = (KW - QW) // 2
ATOMS = 64
EXT = ATOMS + 2 * RIM
HEADS = 4
HEAD = 32
PACK = 80
FAR = -3.0e38
PHASES = (0, 2, 5, 8)
PAIR_ROWS = 8
STEPS = 2


def rank(y, zh, core, zl, x):
    return ((y * N4 + zh) * 2 + core) * 16 + zl * N4 + x


Z_ORDER = ((2, 0),) + tuple(
    (zh, zl) for zh in (0, 1, 3, 2) for zl in range(N4) if (zh, zl) != (2, 0)
)
PLANE_ORDER = (3, 0, 1, 2)
Z_GROUPS = [
    [rank(y, zh, core, zl, x) for zh, zl in Z_ORDER]
    for y in range(N4)
    for core in range(2)
    for x in range(N4)
]
PLANE_GROUPS = [
    [rank(y, zh, core, zl, x) for y in PLANE_ORDER for x in PLANE_ORDER]
    for zh in range(N4)
    for core in range(2)
    for zl in range(N4)
]


def leader(row):
    return jnp.where(row < 16, 4, 8) + lax.rem(row // 2, 4)


ROW_GROUPS = [
    [16 * row + (4 * (1 if row < 16 else 2) + (row // 2) % 4 + j) % 16 for j in range(16)]
    for row in range(32)
]
CORE_GROUPS = [[2 * i, 2 * i + 1] for i in range(16)]


def dot(a, b):
    return jnp.dot(a, b, preferred_element_type=F32)


def iota(shape, dim):
    return lax.broadcasted_iota(jnp.int32, shape, dim)


def layer_norm(values):
    mean = jnp.mean(values, axis=-1, keepdims=True)
    centred = values - mean
    var = jnp.mean(centred * centred, axis=-1, keepdims=True)
    return centred * lax.rsqrt(var + 1e-05)


def band_kernel(
    pair, gain, weight, atoms, token, mask, band, pack,
    tile, gain_v, weight_v, atoms_v, token_v, mask_v, tile_sem, small_sem,
):
    row, col = lax.axis_index("row"), lax.axis_index("col")
    offset = 64 * row - 128 * col
    base = pl.multiple_of(jnp.where(offset >= 64, 48, 0), 16)
    close = (offset >= -64) & (offset <= 128)
    each = pair.shape[0] // STEPS
    big = [
        pltpu.make_async_copy(
            pair.at[pl.ds(each * g, each), pl.ds(base, 80)],
            tile.at[pl.ds(each * g, each)],
            tile_sem.at[g],
        )
        for g in range(STEPS)
    ]

    @pl.when(close)
    def _():
        for copy in big:
            copy.start()

    small = [
        pltpu.make_async_copy(src, dst, small_sem.at[i])
        for i, (src, dst) in enumerate(
            [(gain, gain_v), (weight, weight_v), (atoms, atoms_v), (token, token_v), (mask, mask_v)]
        )
    ]
    for copy in small:
        copy.start()
    band[...] = jnp.zeros_like(band)
    for copy in small:
        copy.wait()
    pack[0:64, :] = atoms_v[...]
    lanes = iota((8, 64), 0)
    local = (token_v[...] - 4 * (row * 16 + col)).astype(F32)
    live = mask_v[...].astype(F32)
    facts = jnp.where(lanes == 0, local, jnp.where(lanes == 1, live, 0.0))
    facts = jnp.concatenate([facts, jnp.zeros_like(facts)], axis=1)
    none = jnp.zeros_like(facts)
    pack[64:80, :] = jnp.concatenate([facts, none], axis=0).astype(BF16)
    first = leader(row)

    def slot(k, low, count):
        return pl.ds(pl.multiple_of(64 * lax.rem(k + 16 - first, 16) + low, 16), count)

    @pl.when(col < 15)
    def _():
        band[slot(col + 1, 0, 48), :] = atoms_v[16:64, :]

    @pl.when(col > 0)
    def _():
        band[slot(col - 1, 0, 48), :] = atoms_v[0:48, :]

    @pl.when(jnp.logical_not(close))
    def _():
        last = jnp.concatenate([none, facts], axis=0).astype(BF16)
        for k in range(16):
            band[64 * k + 48 : 64 * k + 64, :] = last

    @pl.when(close)
    def _():
        half = (iota((8, 128), 1) % 32) // 16
        for g in range(STEPS):
            each = 16 // STEPS
            big[g].wait()
            pieces, inside = [], []
            for k in range(each * g, each * g + each):
                halves = []
                for a in range(2):
                    start = offset + 16 * ((k - 1) // 4 + a)
                    inside.append(((start >= 0) & (start <= 112)).astype(jnp.int32))
                    begin = pl.multiple_of(jnp.clip(start - base, 0, 64), 16)
                    halves.append(tile[4 * k : 4 * k + 4, pl.ds(begin, 16), :])
                pieces.append(jnp.concatenate(halves, axis=1).reshape(128, 128))
            block = jnp.concatenate(pieces, axis=0)
            normed = (layer_norm(block.astype(F32)) * gain_v[...]).astype(BF16)
            table = lax.dot_general(
                weight_v[...], normed, (((1,), (1,)), ((), ())), preferred_element_type=F32
            )
            table = jnp.concatenate([table, jnp.zeros_like(table)], axis=0)
            for j in range(each):
                keep = jnp.where(half == 0, inside[2 * j], inside[2 * j + 1])
                mine = jnp.where(keep > 0, table[:, 128 * j : 128 * j + 128], 0.0)
                last = jnp.concatenate([mine, facts], axis=0).astype(BF16)
                band[slot(each * g + j, 48, 16), :] = last


def atom_kernel(
    band, cross, pack, gain, w_query, w_key, w_value, w_gate, w_out, mid_gain, w_up, w_down,
    w_single, w_row, w_col, _after, atoms_out, terms,
):
    row, col = lax.axis_index("row"), lax.axis_index("col")
    own = pack[...].astype(F32)
    far = cross[...].astype(F32)

    first = leader(row)

    def side(other, low):
        inside = (other >= 0) & (other < 16)
        start = 64 * lax.rem(jnp.clip(other, 0, 15) + 16 - first, 16)
        tile = band[pl.ds(pl.multiple_of(start, 64), 64), :].astype(F32)
        atoms = jnp.where(inside, tile[0:48, :], far[low : low + 48, :])
        return atoms, jnp.where(inside, tile[56:64, :], far[64:72, :])

    left, left_facts = side(col - 1, 16)
    right, right_facts = side(col + 1, 0)
    own_facts = own[64:72, :]
    ext = jnp.concatenate([left, own[0:64, :], right], axis=0)
    normed = (layer_norm(ext) * gain[...]).astype(BF16)
    mine = normed[RIM : RIM + ATOMS, :]
    query = dot(mine, w_query[...]).astype(BF16)
    key = dot(normed, w_key[...]).astype(BF16)
    value = dot(normed, w_value[...]).astype(BF16)
    gate = jax.nn.sigmoid(dot(mine, w_gate[...]))
    head_of = iota((ATOMS, 128), 1) // HEAD
    zero = jnp.zeros_like(query)
    wide = jnp.concatenate([jnp.where(head_of == h, query, zero) for h in range(HEADS)], axis=0)
    logits = lax.dot_general(
        wide, key, (((1,), (1,)), ((), ())), preferred_element_type=F32
    ) * (1.0 / HEAD**0.5)
    lane, spot = iota((128, EXT), 0), iota((128, EXT), 1)

    def moved(facts, low, high, shift):
        pick = (lane >= low) & (lane < high) & (lane + shift == spot)
        return dot(facts.astype(BF16), pick.astype(F32).astype(BF16))

    facts = (
        moved(left_facts, 16, 64, -16)
        + moved(own_facts, 0, 64, RIM)
        + moved(right_facts, 0, 48, RIM + ATOMS)
    )
    where = iota((1, EXT), 1)
    token = facts[0:1, :] + jnp.where(
        where >= RIM + ATOMS, 8.0, jnp.where(where >= RIM, 4.0, 0.0)
    )
    first = (iota((ATOMS, EXT), 0) // QW) * QW
    column = iota((ATOMS, EXT), 1)
    near = (column >= first) & (column < first + KW)
    live = jnp.broadcast_to(facts[1:2, :], (ATOMS, EXT))
    state = jnp.where(near, jnp.where(live > 0.5, 1.0, 0.0), -1.0)
    shift = 4 * lax.rem(col + 3, 4)
    key_pick = ((lane % 32) == token.astype(jnp.int32) + shift).astype(F32).astype(BF16)
    square = iota((ATOMS, 128), 0) == iota((ATOMS, 128), 1)
    own_token = jnp.sum(jnp.where(square, own_facts[0:1, :], 0.0), axis=1, keepdims=True)
    query_pick = (iota((ATOMS, 128), 1) // 32 == own_token.astype(jnp.int32)).astype(F32)

    table = jnp.zeros((16, 128), F32)
    for k in range(16):
        table = table + band[64 * k + 48 : 64 * k + 64, :].astype(F32)
    picked = jnp.concatenate([query_pick * table[h : h + 1, :] for h in range(HEADS)], axis=0)
    bias = dot(picked.astype(BF16), key_pick)
    states = jnp.concatenate([state] * HEADS, axis=0)
    scores = jnp.where(states > 0.5, logits + bias, jnp.where(states > -0.5, -1000000000.0, FAR))
    top = jnp.max(scores, axis=-1, keepdims=True)
    expo = jnp.exp(scores - top)
    weights = (expo / jnp.sum(expo, axis=-1, keepdims=True)).astype(BF16)
    mixed = dot(weights, value)
    attended = jnp.zeros((ATOMS, 128), F32)
    for h in range(HEADS):
        attended = jnp.where(head_of == h, mixed[h * ATOMS : (h + 1) * ATOMS, :], attended)
    gated = (attended * gate).astype(BF16)
    mid = own[0:64, :] + dot(gated, w_out[...])
    mid_norm = (layer_norm(mid) * mid_gain[...]).astype(BF16)
    gate_up = dot(mid_norm, w_up[...])
    width = gate_up.shape[1] // 2
    half = 0.5 * gate_up[:, :width]
    hidden = ((half + half * jnp.tanh(half)) * gate_up[:, width:]).astype(BF16)
    out = (mid + dot(hidden, w_down[...])).astype(BF16)
    atoms_out[...] = out
    single = jnp.maximum(dot(out, w_single[...]), 0.0)
    chosen = jnp.where(
        (iota((8, 128), 0) % 4).astype(F32) == own_facts[0:1, :], own_facts[1:2, :], 0.0
    )[:, 0:64]
    counts = jnp.sum(chosen, axis=-1, keepdims=True)
    chosen = chosen.astype(BF16)
    high = single.astype(BF16)
    low = (single - high.astype(F32)).astype(BF16)
    singles = ((dot(chosen, high) + dot(chosen, low)) / counts).astype(BF16)
    col_terms, row_terms = dot(singles, w_col[...]), dot(singles, w_row[...])
    both = jnp.where(iota((8, 128), 0) < 4, col_terms, row_terms)
    terms[...] = jnp.concatenate([both] * 16, axis=0).astype(BF16)


def spread_kernel(came, _after, going):
    own_zh = lax.rem(lax.axis_index("row") // 2, 4)
    tiles = came[...].astype(F32).reshape(16, 8, 128)
    cols, rows = [], jnp.zeros((16, 128), F32)
    for zh in range(N4):
        group = [tiles[Z_ORDER.index((zh, zl))] for zl in range(N4)]
        cols.append(jnp.concatenate([t[0:4] for t in group], axis=0))
        mine = jnp.concatenate([t[4:8] for t in group], axis=0)
        rows = jnp.where(own_zh == zh, mine, rows)
    plane = jnp.concatenate([piece for x in PLANE_ORDER for piece in (cols[x], rows)], axis=0)
    going[...] = jnp.concatenate([plane] * N4, axis=0).astype(BF16)


def transition_kernel(given, gain, w_up, w_down, _after, out, normed, sem, *, phase):
    low, high = PHASES[phase], PHASES[phase + 1]

    def rows(i):
        return pl.ds(pl.multiple_of(i * PAIR_ROWS, PAIR_ROWS), PAIR_ROWS)

    def norm(i):
        values = out[rows(i)].reshape(-1, 128).astype(F32)
        return (layer_norm(values) * gain[...]).astype(BF16)

    def fetch(i):
        return pltpu.make_async_copy(given.at[rows(i)], out.at[rows(i)], sem.at[i])

    count = PHASES[-1] if phase == 0 else 0
    for i in range(count):
        fetch(i).start()
    for i in range(min(count, 2)):
        fetch(i).wait()
    normed[low % 2] = norm(low)

    @pl.loop(low, high)
    def _(i):
        current = normed[lax.rem(i, 2)]
        following = norm(jnp.minimum(i + 1, high - 1))
        gate_up = dot(current, w_up[...])
        width = gate_up.shape[1] // 2
        half = (0.5 * gate_up[:, :width]).astype(BF16)
        hidden = (half + half * jnp.tanh(half)) * gate_up[:, width:].astype(BF16)
        total = out[rows(i)].reshape(-1, 128).astype(F32) + dot(hidden, w_down[...])
        normed[lax.rem(i + 1, 2)] = following
        out[rows(i)] = total.astype(BF16).reshape(PAIR_ROWS, 128, 128)
        if count:

            @pl.when(i + 2 < count)
            def _():
                fetch(i + 2).wait()

    for i in range(high + 2, count):
        fetch(i).wait()


def add_kernel(part, came, out, done, sem):
    row, col = lax.axis_index("row"), lax.axis_index("col")
    core = lax.rem(row, 2)

    def ordered(start, low):
        piece = came[pl.ds(pl.multiple_of(start, 128), 128), :].astype(F32).reshape(N4, 32, 128)
        return jnp.concatenate(
            [
                piece[PLANE_ORDER.index(x), low + 4 * zl : low + 4 * zl + 4]
                for zl in range(N4)
                for x in range(N4)
            ],
            axis=0,
        )

    zl, y = col // 4, row // 8
    cols = jnp.concatenate(
        [ordered(512 * b + 128 * lax.rem(zl + 1, 4), 0) for b in range(2)], axis=0
    )
    rows = ordered(512 * core + 128 * lax.rem(y + 1, 4), 16)
    copies = []
    for at in range(0, part.shape[0], PAIR_ROWS):
        span = pl.ds(at, PAIR_ROWS)
        total = part[span].astype(F32) + rows[at : at + PAIR_ROWS][:, None, :] + cols[None, :, :]
        done[span] = total.astype(BF16)
        copies.append(pltpu.make_async_copy(done.at[span], out.at[span], sem.at[at // PAIR_ROWS]))
        copies[-1].start()
    for copy in copies:
        copy.wait()


def whole(count):
    return [pl.BlockSpec(memory_space=pltpu.VMEM)] * count


HBM = pl.BlockSpec(memory_space=pltpu.HBM)
ANY = pl.BlockSpec(memory_space=pl.ANY)
SCALARS = pl.BlockSpec(memory_space=pltpu.SMEM)
PARAMS = pltpu.CompilerParams(vmem_limit_bytes=40 * 1024 * 1024)


def cost(flops, moved, trans=0):
    return pl.CostEstimate(flops=flops, bytes_accessed=moved, transcendentals=trans)


def in_hbm(array):
    return pltpu.with_memory_space_constraint(array, pltpu.HBM)


def transition(held, gain, w_up, w_down, phase, after):
    count = 128 * PAIR_ROWS * (PHASES[phase + 1] - PHASES[phase])
    given = HBM if phase == 0 else whole(1)[0]
    return pl.pallas_call(
        functools.partial(transition_kernel, phase=phase),
        in_specs=[given] + whole(3) + [ANY],
        out_specs=whole(1)[0],
        out_shape=jax.ShapeDtypeStruct(held.shape, BF16),
        input_output_aliases={0: 0} if phase else {},
        scratch_shapes=[
            pltpu.VMEM((2, 128 * PAIR_ROWS, 128), BF16),
            pltpu.SemaphoreType.DMA((PHASES[-1],)),
        ],
        compiler_params=PARAMS,
        cost_estimate=cost(count * 4 * 196608, count * 512, count * 512),
    )(held if phase else in_hbm(held), gain, w_up, w_down, after)


def near_diagonal(pair, bias_gain, w_pair_bias, atoms, atom_token, atom_mask):
    return pl.pallas_call(
        band_kernel,
        in_specs=[HBM] * 6,
        out_specs=whole(2),
        out_shape=[
            jax.ShapeDtypeStruct((1024, 128), BF16),
            jax.ShapeDtypeStruct((PACK, 128), BF16),
        ],
        scratch_shapes=[
            pltpu.VMEM((64, 80, 128), BF16),
            pltpu.VMEM((1, 128), F32),
            pltpu.VMEM((4, 128), BF16),
            pltpu.VMEM((64, 128), BF16),
            pltpu.VMEM((1, 64), jnp.int32),
            pltpu.VMEM((1, 64), jnp.int32),
            pltpu.SemaphoreType.DMA((STEPS,)),
            pltpu.SemaphoreType.DMA((5,)),
        ],
        compiler_params=PARAMS,
        cost_estimate=cost(2048 * 2048, 1 << 21),
    )(
        in_hbm(pair),
        in_hbm(bias_gain[None]),
        in_hbm(w_pair_bias.T),
        in_hbm(atoms),
        in_hbm(atom_token[None]),
        in_hbm(atom_mask[None]),
    )


def atom_block(band, cross, pack, gain, w_qkvg, w_out, mid_gain, w_rest, after):
    return pl.pallas_call(
        atom_kernel,
        in_specs=whole(15) + [ANY],
        out_specs=whole(2),
        out_shape=[
            jax.ShapeDtypeStruct((ATOMS, 128), BF16),
            jax.ShapeDtypeStruct((128, 128), BF16),
        ],
        compiler_params=PARAMS,
        cost_estimate=cost(1 << 25, 1 << 20),
    )(band, cross, pack, gain[None], *w_qkvg, w_out, mid_gain[None], *w_rest, after)


def spread_terms(along, after):
    return pl.pallas_call(
        spread_kernel,
        in_specs=whole(1) + [ANY],
        out_specs=whole(1)[0],
        out_shape=jax.ShapeDtypeStruct((512, 128), BF16),
        compiler_params=PARAMS,
    )(along, after)


def add_terms(held, came):
    return pl.pallas_call(
        add_kernel,
        in_specs=whole(2),
        out_specs=HBM,
        out_shape=jax.ShapeDtypeStruct(held.shape, BF16),
        scratch_shapes=[
            pltpu.VMEM(held.shape, BF16),
            pltpu.SemaphoreType.DMA((held.shape[0] // PAIR_ROWS,)),
        ],
        compiler_params=PARAMS,
    )(held, came)


def body(
    pair, atoms, atom_token, atom_mask, bias_gain, w_pair_bias, trans_gain, w_pair_up, w_pair_down,
    atom_gain, w_query, w_key, w_value, w_gate, w_out, mid_gain, w_atom_up, w_atom_down, w_single,
    w_outer_row, w_outer_col,
):
    joint = ("row", "col")
    band, pack = near_diagonal(pair, bias_gain, w_pair_bias, atoms, atom_token, atom_mask)
    band = lax.all_to_all(band, joint, 0, 0, tiled=True, axis_index_groups=ROW_GROUPS)
    ends = [(16 * i + 15, 16 * i + 16) for i in range(31)]
    cross = lax.ppermute(pack, joint, ends + [(j, i) for i, j in ends])
    trans = (trans_gain[None], w_pair_up, w_pair_down)
    held = transition(pair, *trans, 0, pack)
    w_qkvg = (w_query, w_key, w_value, w_gate)
    w_rest = (w_atom_up, w_atom_down, w_single, w_outer_row, w_outer_col)
    atoms_out, terms = atom_block(
        band, cross, pack, atom_gain, w_qkvg, w_out, mid_gain, w_rest, held
    )
    along = lax.all_to_all(terms, joint, 0, 0, tiled=True, axis_index_groups=Z_GROUPS)
    held = transition(held, *trans, 1, terms)
    going = spread_terms(along, held)
    came = lax.all_to_all(going, joint, 0, 0, tiled=True, axis_index_groups=PLANE_GROUPS)
    held = transition(held, *trans, 2, going)
    came, held = lax.optimization_barrier((came, held))
    came = lax.all_gather(came, "row", axis=0, tiled=True, axis_index_groups=CORE_GROUPS)
    return (atoms_out, add_terms(held, came))


def solution(mesh):
    spread = P(("row", "col"))
    in_specs = (P("row", "col", None), P(("row", "col"), None), spread, spread) + (P(),) * 17
    out_specs = (P(("row", "col"), None), P("row", "col", None))
    return jax.shard_map(body, mesh=mesh, in_specs=in_specs, out_specs=out_specs, check_vma=False)
```

```python
import functools

import jax
import jax.numpy as jnp
from jax import lax
from jax.experimental import pallas as pl
from jax.experimental.pallas import tpu as pltpu
from jax.sharding import PartitionSpec as P

F32 = jnp.float32
BF16 = jnp.bfloat16
N4 = 4
QW = 32
KW = 128
RIM = (KW - QW) // 2
ATOMS = 64
EXT = ATOMS + 2 * RIM
HEADS = 4
HEAD = 32
PACK = 80
FAR = -3.0e38
PHASES = (0, 1, 5, 8)
PAIR_ROWS = 8
STEPS = 2


def rank(y, zh, core, zl, x):
    return ((y * N4 + zh) * 2 + core) * 16 + zl * N4 + x


Z_ORDER = ((2, 0),) + tuple(
    (zh, zl) for zh in (0, 1, 3, 2) for zl in range(N4) if (zh, zl) != (2, 0)
)
PLANE_ORDER = (3, 0, 1, 2)
Z_GROUPS = [
    [rank(y, zh, core, zl, x) for zh, zl in Z_ORDER]
    for y in range(N4)
    for core in range(2)
    for x in range(N4)
]
PLANE_GROUPS = [
    [rank(y, zh, core, zl, x) for y in PLANE_ORDER for x in PLANE_ORDER]
    for zh in range(N4)
    for core in range(2)
    for zl in range(N4)
]


def leader(row):
    return jnp.where(row < 16, 4, 8) + lax.rem(row // 2, 4)


ROW_GROUPS = [
    [16 * row + (4 * (1 if row < 16 else 2) + (row // 2) % 4 + j) % 16 for j in range(16)]
    for row in range(32)
]
CORE_GROUPS = [[2 * i, 2 * i + 1] for i in range(16)]


def dot(a, b):
    return jnp.dot(a, b, preferred_element_type=F32)


def iota(shape, dim):
    return lax.broadcasted_iota(jnp.int32, shape, dim)


def layer_norm(values):
    mean = jnp.mean(values, axis=-1, keepdims=True)
    centred = values - mean
    var = jnp.mean(centred * centred, axis=-1, keepdims=True)
    return centred * lax.rsqrt(var + 1e-05)


def band_kernel(
    pair, gain, weight, atoms, token, mask, band, pack,
    tile, gain_v, weight_v, atoms_v, token_v, mask_v, tile_sem, small_sem,
):
    row, col = lax.axis_index("row"), lax.axis_index("col")
    offset = 64 * row - 128 * col
    close = (offset >= -64) & (offset <= 128)
    base = [pl.multiple_of(jnp.clip(offset + 16 * (g - 1), 0, 80), 16) for g in range(4)]
    big = [
        pltpu.make_async_copy(
            pair.at[pl.ds(16 * g, 16), pl.ds(base[g], 48)],
            tile.at[pl.ds(16 * g, 16)],
            tile_sem.at[g],
        )
        for g in range(4)
    ]

    @pl.when(close)
    def _():
        for copy in big:
            copy.start()

    small = [
        pltpu.make_async_copy(src, dst, small_sem.at[i])
        for i, (src, dst) in enumerate(
            [(gain, gain_v), (weight, weight_v), (atoms, atoms_v), (token, token_v), (mask, mask_v)]
        )
    ]
    for copy in small:
        copy.start()
    band[...] = jnp.zeros_like(band)
    for copy in small:
        copy.wait()
    pack[0:64, :] = atoms_v[...]
    lanes = iota((8, 64), 0)
    local = (token_v[...] - 4 * (row * 16 + col)).astype(F32)
    live = mask_v[...].astype(F32)
    facts = jnp.where(lanes == 0, local, jnp.where(lanes == 1, live, 0.0))
    facts = jnp.concatenate([facts, jnp.zeros_like(facts)], axis=1)
    none = jnp.zeros_like(facts)
    pack[64:80, :] = jnp.concatenate([facts, none], axis=0).astype(BF16)
    first = leader(row)

    def slot(k, low, count):
        return pl.ds(pl.multiple_of(64 * lax.rem(k + 16 - first, 16) + low, 16), count)

    @pl.when(col < 15)
    def _():
        band[slot(col + 1, 0, 48), :] = atoms_v[16:64, :]

    @pl.when(col > 0)
    def _():
        band[slot(col - 1, 0, 48), :] = atoms_v[0:48, :]

    @pl.when(jnp.logical_not(close))
    def _():
        last = jnp.concatenate([none, facts], axis=0).astype(BF16)
        for k in range(16):
            band[64 * k + 48 : 64 * k + 64, :] = last

    @pl.when(close)
    def _():
        half = (iota((8, 128), 1) % 32) // 16
        for g in range(STEPS):
            each = 16 // STEPS
            for copy in big[4 // STEPS * g : 4 // STEPS * (g + 1)]:
                copy.wait()
            pieces, inside = [], []
            for k in range(each * g, each * g + each):
                halves = []
                for a in range(2):
                    start = offset + 16 * ((k - 1) // 4 + a)
                    inside.append(((start >= 0) & (start <= 112)).astype(jnp.int32))
                    begin = pl.multiple_of(jnp.clip(start - base[k // 4], 0, 32), 16)
                    halves.append(tile[4 * k : 4 * k + 4, pl.ds(begin, 16), :])
                pieces.append(jnp.concatenate(halves, axis=1).reshape(128, 128))
            block = jnp.concatenate(pieces, axis=0)
            normed = (layer_norm(block.astype(F32)) * gain_v[...]).astype(BF16)
            table = lax.dot_general(
                weight_v[...], normed, (((1,), (1,)), ((), ())), preferred_element_type=F32
            )
            table = jnp.concatenate([table, jnp.zeros_like(table)], axis=0)
            for j in range(each):
                keep = jnp.where(half == 0, inside[2 * j], inside[2 * j + 1])
                mine = jnp.where(keep > 0, table[:, 128 * j : 128 * j + 128], 0.0)
                last = jnp.concatenate([mine, facts], axis=0).astype(BF16)
                band[slot(each * g + j, 48, 16), :] = last


def atom_kernel(
    band, cross, pack, gain, w_query, w_key, w_value, w_gate, w_out, mid_gain, w_up, w_down,
    w_single, w_row, w_col, _after, atoms_out, terms,
):
    row, col = lax.axis_index("row"), lax.axis_index("col")
    own = pack[...].astype(F32)
    far = cross[...].astype(F32)

    first = leader(row)

    def side(other, low):
        inside = (other >= 0) & (other < 16)
        start = 64 * lax.rem(jnp.clip(other, 0, 15) + 16 - first, 16)
        tile = band[pl.ds(pl.multiple_of(start, 64), 64), :].astype(F32)
        atoms = jnp.where(inside, tile[0:48, :], far[low : low + 48, :])
        return atoms, jnp.where(inside, tile[56:64, :], far[64:72, :])

    left, left_facts = side(col - 1, 16)
    right, right_facts = side(col + 1, 0)
    own_facts = own[64:72, :]
    ext = jnp.concatenate([left, own[0:64, :], right], axis=0)
    normed = (layer_norm(ext) * gain[...]).astype(BF16)
    mine = normed[RIM : RIM + ATOMS, :]
    query = dot(mine, w_query[...]).astype(BF16)
    key = dot(normed, w_key[...]).astype(BF16)
    value = dot(normed, w_value[...]).astype(BF16)
    gate = jax.nn.sigmoid(dot(mine, w_gate[...]))
    head_of = iota((ATOMS, 128), 1) // HEAD
    zero = jnp.zeros_like(query)
    wide = jnp.concatenate([jnp.where(head_of == h, query, zero) for h in range(HEADS)], axis=0)
    logits = lax.dot_general(
        wide, key, (((1,), (1,)), ((), ())), preferred_element_type=F32
    ) * (1.0 / HEAD**0.5)
    lane, spot = iota((128, EXT), 0), iota((128, EXT), 1)

    def moved(facts, low, high, shift):
        pick = (lane >= low) & (lane < high) & (lane + shift == spot)
        return dot(facts.astype(BF16), pick.astype(F32).astype(BF16))

    facts = (
        moved(left_facts, 16, 64, -16)
        + moved(own_facts, 0, 64, RIM)
        + moved(right_facts, 0, 48, RIM + ATOMS)
    )
    where = iota((1, EXT), 1)
    token = facts[0:1, :] + jnp.where(
        where >= RIM + ATOMS, 8.0, jnp.where(where >= RIM, 4.0, 0.0)
    )
    first = (iota((ATOMS, EXT), 0) // QW) * QW
    column = iota((ATOMS, EXT), 1)
    near = (column >= first) & (column < first + KW)
    live = jnp.broadcast_to(facts[1:2, :], (ATOMS, EXT))
    state = jnp.where(near, jnp.where(live > 0.5, 1.0, 0.0), -1.0)
    shift = 4 * lax.rem(col + 3, 4)
    key_pick = ((lane % 32) == token.astype(jnp.int32) + shift).astype(F32).astype(BF16)
    square = iota((ATOMS, 128), 0) == iota((ATOMS, 128), 1)
    own_token = jnp.sum(jnp.where(square, own_facts[0:1, :], 0.0), axis=1, keepdims=True)
    query_pick = (iota((ATOMS, 128), 1) // 32 == own_token.astype(jnp.int32)).astype(F32)

    table = jnp.zeros((16, 128), F32)
    for k in range(16):
        table = table + band[64 * k + 48 : 64 * k + 64, :].astype(F32)
    picked = jnp.concatenate([query_pick * table[h : h + 1, :] for h in range(HEADS)], axis=0)
    bias = dot(picked.astype(BF16), key_pick)
    states = jnp.concatenate([state] * HEADS, axis=0)
    scores = jnp.where(states > 0.5, logits + bias, jnp.where(states > -0.5, -1000000000.0, FAR))
    top = jnp.max(scores, axis=-1, keepdims=True)
    expo = jnp.exp(scores - top)
    mixed = dot(expo.astype(BF16), value) / jnp.sum(expo, axis=-1, keepdims=True)
    attended = jnp.zeros((ATOMS, 128), F32)
    for h in range(HEADS):
        attended = jnp.where(head_of == h, mixed[h * ATOMS : (h + 1) * ATOMS, :], attended)
    gated = (attended * gate).astype(BF16)
    mid = own[0:64, :] + dot(gated, w_out[...])
    mid_norm = (layer_norm(mid) * mid_gain[...]).astype(BF16)
    gate_up = dot(mid_norm, w_up[...])
    width = gate_up.shape[1] // 2
    half = 0.5 * gate_up[:, :width]
    hidden = ((half + half * jnp.tanh(half)) * gate_up[:, width:]).astype(BF16)
    out = (mid + dot(hidden, w_down[...])).astype(BF16)
    atoms_out[...] = out
    single = jnp.maximum(dot(out, w_single[...]), 0.0)
    chosen = jnp.where(
        (iota((8, 128), 0) % 4).astype(F32) == own_facts[0:1, :], own_facts[1:2, :], 0.0
    )[:, 0:64]
    counts = jnp.sum(chosen, axis=-1, keepdims=True)
    high = single.astype(BF16)
    parts = jnp.concatenate([high, (single - high.astype(F32)).astype(BF16)], axis=0)
    twice = jnp.concatenate([chosen, chosen], axis=1).astype(BF16)
    singles = (dot(twice, parts) / counts).astype(BF16)
    col_terms, row_terms = dot(singles, w_col[...]), dot(singles, w_row[...])
    both = jnp.where(iota((8, 128), 0) < 4, col_terms, row_terms)
    terms[...] = jnp.concatenate([both] * 16, axis=0).astype(BF16)


def spread_kernel(came, _after, going):
    own_zh = lax.rem(lax.axis_index("row") // 2, 4)
    tiles = came[...].astype(F32).reshape(16, 8, 128)
    cols, rows = [], jnp.zeros((16, 128), F32)
    for zh in range(N4):
        group = [tiles[Z_ORDER.index((zh, zl))] for zl in range(N4)]
        cols.append(jnp.concatenate([t[0:4] for t in group], axis=0))
        mine = jnp.concatenate([t[4:8] for t in group], axis=0)
        rows = jnp.where(own_zh == zh, mine, rows)
    plane = jnp.concatenate([piece for x in PLANE_ORDER for piece in (cols[x], rows)], axis=0)
    plane = plane.astype(BF16)
    for y in range(N4):
        going[128 * y : 128 * y + 128, :] = plane


def transition_kernel(given, gain, w_up, w_down, _after, out, normed, sem, *, phase):
    low, high = PHASES[phase], PHASES[phase + 1]

    def rows(i):
        return pl.ds(pl.multiple_of(i * PAIR_ROWS, PAIR_ROWS), PAIR_ROWS)

    def norm(i):
        values = out[rows(i)].reshape(-1, 128).astype(F32)
        return (layer_norm(values) * gain[...]).astype(BF16)

    def fetch(i):
        return pltpu.make_async_copy(given.at[rows(i)], out.at[rows(i)], sem.at[i])

    count = PHASES[-1] if phase == 0 else 0
    for i in range(count):
        fetch(i).start()
    for i in range(min(count, 2)):
        fetch(i).wait()
    normed[low % 2] = norm(low)

    @pl.loop(low, high)
    def _(i):
        current = normed[lax.rem(i, 2)]
        following = norm(jnp.minimum(i + 1, high - 1))
        gate_up = dot(current, w_up[...])
        width = gate_up.shape[1] // 2
        half = (0.5 * gate_up[:, :width]).astype(BF16)
        hidden = (half + half * jnp.tanh(half)) * gate_up[:, width:].astype(BF16)
        total = out[rows(i)].reshape(-1, 128).astype(F32) + dot(hidden, w_down[...])
        normed[lax.rem(i + 1, 2)] = following
        out[rows(i)] = total.astype(BF16).reshape(PAIR_ROWS, 128, 128)
        if count:

            @pl.when(i + 2 < count)
            def _():
                fetch(i + 2).wait()

    for i in range(high + 2, count):
        fetch(i).wait()


def add_kernel(part, came, out, done, sem):
    row, col = lax.axis_index("row"), lax.axis_index("col")
    core = lax.rem(row, 2)

    def ordered(start, low):
        piece = came[pl.ds(pl.multiple_of(start, 128), 128), :].astype(F32).reshape(N4, 32, 128)
        return jnp.concatenate(
            [
                piece[PLANE_ORDER.index(x), low + 4 * zl : low + 4 * zl + 4]
                for zl in range(N4)
                for x in range(N4)
            ],
            axis=0,
        )

    zl, y = col // 4, row // 8
    cols = jnp.concatenate(
        [ordered(512 * b + 128 * lax.rem(zl + 1, 4), 0) for b in range(2)], axis=0
    )
    rows = ordered(512 * core + 128 * lax.rem(y + 1, 4), 16)
    copies = []
    for at in range(0, part.shape[0], PAIR_ROWS):
        span = pl.ds(at, PAIR_ROWS)
        total = part[span].astype(F32) + rows[at : at + PAIR_ROWS][:, None, :] + cols[None, :, :]
        done[span] = total.astype(BF16)
        copies.append(pltpu.make_async_copy(done.at[span], out.at[span], sem.at[at // PAIR_ROWS]))
        copies[-1].start()
    for copy in copies:
        copy.wait()


def whole(count):
    return [pl.BlockSpec(memory_space=pltpu.VMEM)] * count


HBM = pl.BlockSpec(memory_space=pltpu.HBM)
ANY = pl.BlockSpec(memory_space=pl.ANY)
SCALARS = pl.BlockSpec(memory_space=pltpu.SMEM)
PARAMS = pltpu.CompilerParams(vmem_limit_bytes=40 * 1024 * 1024)


def cost(flops, moved, trans=0):
    return pl.CostEstimate(flops=flops, bytes_accessed=moved, transcendentals=trans)


def in_hbm(array):
    return pltpu.with_memory_space_constraint(array, pltpu.HBM)


def transition(held, gain, w_up, w_down, phase, after):
    count = 128 * PAIR_ROWS * (PHASES[phase + 1] - PHASES[phase])
    given = HBM if phase == 0 else whole(1)[0]
    return pl.pallas_call(
        functools.partial(transition_kernel, phase=phase),
        in_specs=[given] + whole(3) + [ANY],
        out_specs=whole(1)[0],
        out_shape=jax.ShapeDtypeStruct(held.shape, BF16),
        input_output_aliases={0: 0} if phase else {},
        scratch_shapes=[
            pltpu.VMEM((2, 128 * PAIR_ROWS, 128), BF16),
            pltpu.SemaphoreType.DMA((PHASES[-1],)),
        ],
        compiler_params=PARAMS,
        cost_estimate=cost(count * 4 * 196608, count * 512, count * 512),
    )(held if phase else in_hbm(held), gain, w_up, w_down, after)


def near_diagonal(pair, bias_gain, w_pair_bias, atoms, atom_token, atom_mask):
    return pl.pallas_call(
        band_kernel,
        in_specs=[HBM] * 6,
        out_specs=whole(2),
        out_shape=[
            jax.ShapeDtypeStruct((1024, 128), BF16),
            jax.ShapeDtypeStruct((PACK, 128), BF16),
        ],
        scratch_shapes=[
            pltpu.VMEM((64, 48, 128), BF16),
            pltpu.VMEM((1, 128), F32),
            pltpu.VMEM((4, 128), BF16),
            pltpu.VMEM((64, 128), BF16),
            pltpu.VMEM((1, 64), jnp.int32),
            pltpu.VMEM((1, 64), jnp.int32),
            pltpu.SemaphoreType.DMA((4,)),
            pltpu.SemaphoreType.DMA((5,)),
        ],
        compiler_params=PARAMS,
        cost_estimate=cost(2048 * 2048, 1 << 21),
    )(
        in_hbm(pair),
        in_hbm(bias_gain[None]),
        in_hbm(w_pair_bias.T),
        in_hbm(atoms),
        in_hbm(atom_token[None]),
        in_hbm(atom_mask[None]),
    )


def atom_block(band, cross, pack, gain, w_qkvg, w_out, mid_gain, w_rest, after):
    return pl.pallas_call(
        atom_kernel,
        in_specs=whole(15) + [ANY],
        out_specs=whole(2),
        out_shape=[
            jax.ShapeDtypeStruct((ATOMS, 128), BF16),
            jax.ShapeDtypeStruct((128, 128), BF16),
        ],
        compiler_params=PARAMS,
        cost_estimate=cost(1 << 25, 1 << 20),
    )(band, cross, pack, gain[None], *w_qkvg, w_out, mid_gain[None], *w_rest, after)


def spread_terms(along, after):
    return pl.pallas_call(
        spread_kernel,
        in_specs=whole(1) + [ANY],
        out_specs=whole(1)[0],
        out_shape=jax.ShapeDtypeStruct((512, 128), BF16),
        compiler_params=PARAMS,
    )(along, after)


def add_terms(held, came):
    return pl.pallas_call(
        add_kernel,
        in_specs=whole(2),
        out_specs=HBM,
        out_shape=jax.ShapeDtypeStruct(held.shape, BF16),
        scratch_shapes=[
            pltpu.VMEM(held.shape, BF16),
            pltpu.SemaphoreType.DMA((held.shape[0] // PAIR_ROWS,)),
        ],
        compiler_params=PARAMS,
    )(held, came)


def body(
    pair, atoms, atom_token, atom_mask, bias_gain, w_pair_bias, trans_gain, w_pair_up, w_pair_down,
    atom_gain, w_query, w_key, w_value, w_gate, w_out, mid_gain, w_atom_up, w_atom_down, w_single,
    w_outer_row, w_outer_col,
):
    joint = ("row", "col")
    band, pack = near_diagonal(pair, bias_gain, w_pair_bias, atoms, atom_token, atom_mask)
    band = lax.all_to_all(band, joint, 0, 0, tiled=True, axis_index_groups=ROW_GROUPS)
    ends = [(16 * i + 15, 16 * i + 16) for i in range(31)]
    cross = lax.ppermute(pack, joint, ends + [(j, i) for i, j in ends])
    trans = (trans_gain[None], w_pair_up, w_pair_down)
    held = transition(pair, *trans, 0, pack)
    w_qkvg = (w_query, w_key, w_value, w_gate)
    w_rest = (w_atom_up, w_atom_down, w_single, w_outer_row, w_outer_col)
    atoms_out, terms = atom_block(
        band, cross, pack, atom_gain, w_qkvg, w_out, mid_gain, w_rest, held
    )
    along = lax.all_to_all(terms, joint, 0, 0, tiled=True, axis_index_groups=Z_GROUPS)
    held = transition(held, *trans, 1, terms)
    going = spread_terms(along, held)
    came = lax.all_to_all(going, joint, 0, 0, tiled=True, axis_index_groups=PLANE_GROUPS)
    held = transition(held, *trans, 2, going)
    came, held = lax.optimization_barrier((came, held))
    came = lax.all_gather(came, "row", axis=0, tiled=True, axis_index_groups=CORE_GROUPS)
    return (atoms_out, add_terms(held, came))


def solution(mesh):
    spread = P(("row", "col"))
    in_specs = (P("row", "col", None), P(("row", "col"), None), spread, spread) + (P(),) * 17
    out_specs = (P(("row", "col"), None), P("row", "col", None))
    return jax.shard_map(body, mesh=mesh, in_specs=in_specs, out_specs=out_specs, check_vma=False)
```

```python
import functools

import jax
import jax.numpy as jnp
from jax import lax
from jax.experimental import pallas as pl
from jax.experimental.pallas import tpu as pltpu
from jax.sharding import PartitionSpec as P

F32 = jnp.float32
BF16 = jnp.bfloat16
N4 = 4
QW = 32
KW = 128
RIM = (KW - QW) // 2
ATOMS = 64
EXT = ATOMS + 2 * RIM
HEADS = 4
HEAD = 32
PACK = 80
FAR = -3.0e38
PHASES = (0, 2, 5, 8)
PAIR_ROWS = 8
STEPS = 2


def rank(y, zh, core, zl, x):
    return ((y * N4 + zh) * 2 + core) * 16 + zl * N4 + x


Z_ORDER = ((2, 1),) + tuple(
    (zh, zl) for zh in (0, 1, 3, 2) for zl in range(N4) if (zh, zl) != (2, 1)
)
PLANE_ORDER = (3, 0, 1, 2)
Z_GROUPS = [
    [rank(y, zh, core, zl, x) for zh, zl in Z_ORDER]
    for y in range(N4)
    for core in range(2)
    for x in range(N4)
]
PLANE_GROUPS = [
    [rank(y, zh, core, zl, x) for y in PLANE_ORDER for x in PLANE_ORDER]
    for zh in range(N4)
    for core in range(2)
    for zl in range(N4)
]


def leader(row):
    return jnp.where(row < 16, 4, 8) + lax.rem(row // 2, 4)


ROW_GROUPS = [
    [16 * row + (4 * (1 if row < 16 else 2) + (row // 2) % 4 + j) % 16 for j in range(16)]
    for row in range(32)
]
CORE_GROUPS = [[2 * i, 2 * i + 1] for i in range(16)]


def dot(a, b):
    return jnp.dot(a, b, preferred_element_type=F32)


def iota(shape, dim):
    return lax.broadcasted_iota(jnp.int32, shape, dim)


def layer_norm(values):
    mean = jnp.mean(values, axis=-1, keepdims=True)
    centred = values - mean
    var = jnp.mean(centred * centred, axis=-1, keepdims=True)
    return centred * lax.rsqrt(var + 1e-05)


def band_kernel(
    pair, gain, weight, atoms, token, mask, band, pack,
    tile, gain_v, weight_v, atoms_v, token_v, mask_v, tile_sem, small_sem,
):
    row, col = lax.axis_index("row"), lax.axis_index("col")
    offset = 64 * row - 128 * col
    close = (offset >= -64) & (offset <= 128)
    base = [pl.multiple_of(jnp.clip(offset + 16 * (g - 1), 0, 80), 16) for g in range(4)]
    big = [
        pltpu.make_async_copy(
            pair.at[pl.ds(16 * g, 16), pl.ds(base[g], 48)],
            tile.at[pl.ds(16 * g, 16)],
            tile_sem.at[g],
        )
        for g in range(4)
    ]

    @pl.when(close)
    def _():
        for copy in big:
            copy.start()

    small = [
        pltpu.make_async_copy(src, dst, small_sem.at[i])
        for i, (src, dst) in enumerate(
            [(gain, gain_v), (weight, weight_v), (atoms, atoms_v), (token, token_v), (mask, mask_v)]
        )
    ]
    for copy in small:
        copy.start()
    band[...] = jnp.zeros_like(band)
    for copy in small:
        copy.wait()
    pack[0:64, :] = atoms_v[...]
    lanes = iota((8, 64), 0)
    local = (token_v[...] - 4 * (row * 16 + col)).astype(F32)
    live = mask_v[...].astype(F32)
    facts = jnp.where(lanes == 0, local, jnp.where(lanes == 1, live, 0.0))
    facts = jnp.concatenate([facts, jnp.zeros_like(facts)], axis=1)
    none = jnp.zeros_like(facts)
    pack[64:80, :] = jnp.concatenate([facts, none], axis=0).astype(BF16)
    first = leader(row)

    def slot(k, low, count):
        return pl.ds(pl.multiple_of(64 * lax.rem(k + 16 - first, 16) + low, 16), count)

    @pl.when(col < 15)
    def _():
        band[slot(col + 1, 0, 48), :] = atoms_v[16:64, :]

    @pl.when(col > 0)
    def _():
        band[slot(col - 1, 0, 48), :] = atoms_v[0:48, :]

    @pl.when(jnp.logical_not(close))
    def _():
        last = jnp.concatenate([none, facts], axis=0).astype(BF16)
        for k in range(16):
            band[64 * k + 48 : 64 * k + 64, :] = last

    @pl.when(close)
    def _():
        half = (iota((8, 128), 1) % 32) // 16
        for g in range(STEPS):
            each = 16 // STEPS
            for copy in big[4 // STEPS * g : 4 // STEPS * (g + 1)]:
                copy.wait()
            pieces, inside = [], []
            for k in range(each * g, each * g + each):
                halves = []
                for a in range(2):
                    start = offset + 16 * ((k - 1) // 4 + a)
                    inside.append(((start >= 0) & (start <= 112)).astype(jnp.int32))
                    begin = pl.multiple_of(jnp.clip(start - base[k // 4], 0, 32), 16)
                    halves.append(tile[4 * k : 4 * k + 4, pl.ds(begin, 16), :])
                pieces.append(jnp.concatenate(halves, axis=1).reshape(128, 128))
            block = jnp.concatenate(pieces, axis=0)
            normed = (layer_norm(block.astype(F32)) * gain_v[...]).astype(BF16)
            table = lax.dot_general(
                weight_v[...], normed, (((1,), (1,)), ((), ())), preferred_element_type=F32
            )
            table = jnp.concatenate([table, jnp.zeros_like(table)], axis=0)
            for j in range(each):
                keep = jnp.where(half == 0, inside[2 * j], inside[2 * j + 1])
                mine = jnp.where(keep > 0, table[:, 128 * j : 128 * j + 128], 0.0)
                last = jnp.concatenate([mine, facts], axis=0).astype(BF16)
                band[slot(each * g + j, 48, 16), :] = last


def atom_kernel(
    band, cross, pack, gain, w_query, w_key, w_value, w_gate, w_out, mid_gain, w_up, w_down,
    w_single, w_row, w_col, _after, atoms_out, terms,
):
    row, col = lax.axis_index("row"), lax.axis_index("col")
    own = pack[...].astype(F32)
    far = cross[...].astype(F32)

    first = leader(row)

    def side(other, low):
        inside = (other >= 0) & (other < 16)
        start = 64 * lax.rem(jnp.clip(other, 0, 15) + 16 - first, 16)
        tile = band[pl.ds(pl.multiple_of(start, 64), 64), :].astype(F32)
        atoms = jnp.where(inside, tile[0:48, :], far[low : low + 48, :])
        return atoms, jnp.where(inside, tile[56:64, :], far[64:72, :])

    left, left_facts = side(col - 1, 16)
    right, right_facts = side(col + 1, 0)
    own_facts = own[64:72, :]
    ext = jnp.concatenate([left, own[0:64, :], right], axis=0)
    normed = (layer_norm(ext) * gain[...]).astype(BF16)
    mine = normed[RIM : RIM + ATOMS, :]
    query = dot(mine, w_query[...]).astype(BF16)
    key = dot(normed, w_key[...]).astype(BF16)
    value = dot(normed, w_value[...]).astype(BF16)
    gate = jax.nn.sigmoid(dot(mine, w_gate[...]))
    head_of = iota((ATOMS, 128), 1) // HEAD
    zero = jnp.zeros_like(query)
    wide = jnp.concatenate([jnp.where(head_of == h, query, zero) for h in range(HEADS)], axis=0)
    logits = lax.dot_general(
        wide, key, (((1,), (1,)), ((), ())), preferred_element_type=F32
    ) * (1.0 / HEAD**0.5)
    lane, spot = iota((128, EXT), 0), iota((128, EXT), 1)

    def moved(facts, low, high, shift):
        pick = (lane >= low) & (lane < high) & (lane + shift == spot)
        return dot(facts.astype(BF16), pick.astype(F32).astype(BF16))

    facts = (
        moved(left_facts, 16, 64, -16)
        + moved(own_facts, 0, 64, RIM)
        + moved(right_facts, 0, 48, RIM + ATOMS)
    )
    where = iota((1, EXT), 1)
    token = facts[0:1, :] + jnp.where(
        where >= RIM + ATOMS, 8.0, jnp.where(where >= RIM, 4.0, 0.0)
    )
    first = (iota((ATOMS, EXT), 0) // QW) * QW
    column = iota((ATOMS, EXT), 1)
    near = (column >= first) & (column < first + KW)
    live = jnp.broadcast_to(facts[1:2, :], (ATOMS, EXT))
    state = jnp.where(near, jnp.where(live > 0.5, 1.0, 0.0), -1.0)
    shift = 4 * lax.rem(col + 3, 4)
    key_pick = ((lane % 32) == token.astype(jnp.int32) + shift).astype(F32).astype(BF16)
    square = iota((ATOMS, 128), 0) == iota((ATOMS, 128), 1)
    own_token = jnp.sum(jnp.where(square, own_facts[0:1, :], 0.0), axis=1, keepdims=True)
    query_pick = (iota((ATOMS, 128), 1) // 32 == own_token.astype(jnp.int32)).astype(F32)

    table = jnp.zeros((16, 128), F32)
    for k in range(16):
        table = table + band[64 * k + 48 : 64 * k + 64, :].astype(F32)
    picked = jnp.concatenate([query_pick * table[h : h + 1, :] for h in range(HEADS)], axis=0)
    bias = dot(picked.astype(BF16), key_pick)
    states = jnp.concatenate([state] * HEADS, axis=0)
    scores = jnp.where(states > 0.5, logits + bias, jnp.where(states > -0.5, -1000000000.0, FAR))
    top = jnp.max(scores, axis=-1, keepdims=True)
    expo = jnp.exp(scores - top)
    mixed = dot(expo.astype(BF16), value) / jnp.sum(expo, axis=-1, keepdims=True)
    attended = jnp.zeros((ATOMS, 128), F32)
    for h in range(HEADS):
        attended = jnp.where(head_of == h, mixed[h * ATOMS : (h + 1) * ATOMS, :], attended)
    gated = (attended * gate).astype(BF16)
    mid = own[0:64, :] + dot(gated, w_out[...])
    mid_norm = (layer_norm(mid) * mid_gain[...]).astype(BF16)
    gate_up = dot(mid_norm, w_up[...])
    width = gate_up.shape[1] // 2
    half = 0.5 * gate_up[:, :width]
    hidden = ((half + half * jnp.tanh(half)) * gate_up[:, width:]).astype(BF16)
    out = (mid + dot(hidden, w_down[...])).astype(BF16)
    atoms_out[...] = out
    single = jnp.maximum(dot(out, w_single[...]), 0.0)
    chosen = jnp.where(
        (iota((8, 128), 0) % 4).astype(F32) == own_facts[0:1, :], own_facts[1:2, :], 0.0
    )[:, 0:64]
    counts = jnp.sum(chosen, axis=-1, keepdims=True)
    high = single.astype(BF16)
    parts = jnp.concatenate([high, (single - high.astype(F32)).astype(BF16)], axis=0)
    twice = jnp.concatenate([chosen, chosen], axis=1).astype(BF16)
    singles = (dot(twice, parts) / counts).astype(BF16)
    col_terms, row_terms = dot(singles, w_col[...]), dot(singles, w_row[...])
    both = jnp.where(iota((8, 128), 0) < 4, col_terms, row_terms)
    terms[...] = jnp.concatenate([both] * 16, axis=0).astype(BF16)


def spread_kernel(came, _after, going):
    own_zh = lax.rem(lax.axis_index("row") // 2, 4)
    tiles = came[...].astype(F32).reshape(16, 8, 128)
    cols, rows = [], jnp.zeros((16, 128), F32)
    for zh in range(N4):
        group = [tiles[Z_ORDER.index((zh, zl))] for zl in range(N4)]
        cols.append(jnp.concatenate([t[0:4] for t in group], axis=0))
        mine = jnp.concatenate([t[4:8] for t in group], axis=0)
        rows = jnp.where(own_zh == zh, mine, rows)
    plane = jnp.concatenate([piece for x in PLANE_ORDER for piece in (cols[x], rows)], axis=0)
    plane = plane.astype(BF16)
    for y in range(N4):
        going[128 * y : 128 * y + 128, :] = plane


def transition_kernel(given, gain, w_up, w_down, _after, out, normed, sem, *, phase):
    low, high = PHASES[phase], PHASES[phase + 1]

    def rows(i):
        return pl.ds(pl.multiple_of(i * PAIR_ROWS, PAIR_ROWS), PAIR_ROWS)

    def norm(i):
        values = out[rows(i)].reshape(-1, 128).astype(F32)
        return (layer_norm(values) * gain[...]).astype(BF16)

    def fetch(i):
        return pltpu.make_async_copy(given.at[rows(i)], out.at[rows(i)], sem.at[i])

    count = PHASES[-1] if phase == 0 else 0
    for i in range(count):
        fetch(i).start()
    for i in range(min(count, 2)):
        fetch(i).wait()
    normed[low % 2] = norm(low)

    @pl.loop(low, high)
    def _(i):
        current = normed[lax.rem(i, 2)]
        following = norm(jnp.minimum(i + 1, high - 1))
        gate_up = dot(current, w_up[...])
        width = gate_up.shape[1] // 2
        half = (0.5 * gate_up[:, :width]).astype(BF16)
        hidden = (half + half * jnp.tanh(half)) * gate_up[:, width:].astype(BF16)
        total = out[rows(i)].reshape(-1, 128).astype(F32) + dot(hidden, w_down[...])
        normed[lax.rem(i + 1, 2)] = following
        out[rows(i)] = total.astype(BF16).reshape(PAIR_ROWS, 128, 128)
        if count:

            @pl.when(i + 2 < count)
            def _():
                fetch(i + 2).wait()

    for i in range(high + 2, count):
        fetch(i).wait()


def add_kernel(part, came, out, done, sem):
    row, col = lax.axis_index("row"), lax.axis_index("col")
    core = lax.rem(row, 2)

    def ordered(start, low):
        piece = came[pl.ds(pl.multiple_of(start, 128), 128), :].astype(F32).reshape(N4, 32, 128)
        return jnp.concatenate(
            [
                piece[PLANE_ORDER.index(x), low + 4 * zl : low + 4 * zl + 4]
                for zl in range(N4)
                for x in range(N4)
            ],
            axis=0,
        )

    zl, y = col // 4, row // 8
    cols = jnp.concatenate(
        [ordered(512 * b + 128 * lax.rem(zl + 1, 4), 0) for b in range(2)], axis=0
    )
    rows = ordered(512 * core + 128 * lax.rem(y + 1, 4), 16)
    copies = []
    for at in range(0, part.shape[0], PAIR_ROWS):
        span = pl.ds(at, PAIR_ROWS)
        total = part[span].astype(F32) + rows[at : at + PAIR_ROWS][:, None, :] + cols[None, :, :]
        done[span] = total.astype(BF16)
        copies.append(pltpu.make_async_copy(done.at[span], out.at[span], sem.at[at // PAIR_ROWS]))
        copies[-1].start()
    for copy in copies:
        copy.wait()


def whole(count):
    return [pl.BlockSpec(memory_space=pltpu.VMEM)] * count


HBM = pl.BlockSpec(memory_space=pltpu.HBM)
ANY = pl.BlockSpec(memory_space=pl.ANY)
SCALARS = pl.BlockSpec(memory_space=pltpu.SMEM)
PARAMS = pltpu.CompilerParams(vmem_limit_bytes=40 * 1024 * 1024)


def cost(flops, moved, trans=0):
    return pl.CostEstimate(flops=flops, bytes_accessed=moved, transcendentals=trans)


def in_hbm(array):
    return pltpu.with_memory_space_constraint(array, pltpu.HBM)


def transition(held, gain, w_up, w_down, phase, after):
    count = 128 * PAIR_ROWS * (PHASES[phase + 1] - PHASES[phase])
    given = HBM if phase == 0 else whole(1)[0]
    return pl.pallas_call(
        functools.partial(transition_kernel, phase=phase),
        in_specs=[given] + whole(3) + [ANY],
        out_specs=whole(1)[0],
        out_shape=jax.ShapeDtypeStruct(held.shape, BF16),
        input_output_aliases={0: 0} if phase else {},
        scratch_shapes=[
            pltpu.VMEM((2, 128 * PAIR_ROWS, 128), BF16),
            pltpu.SemaphoreType.DMA((PHASES[-1],)),
        ],
        compiler_params=PARAMS,
        cost_estimate=cost(count * 4 * 196608, count * 512, count * 512),
    )(held if phase else in_hbm(held), gain, w_up, w_down, after)


def near_diagonal(pair, bias_gain, w_pair_bias, atoms, atom_token, atom_mask):
    return pl.pallas_call(
        band_kernel,
        in_specs=[HBM] * 6,
        out_specs=whole(2),
        out_shape=[
            jax.ShapeDtypeStruct((1024, 128), BF16),
            jax.ShapeDtypeStruct((PACK, 128), BF16),
        ],
        scratch_shapes=[
            pltpu.VMEM((64, 48, 128), BF16),
            pltpu.VMEM((1, 128), F32),
            pltpu.VMEM((4, 128), BF16),
            pltpu.VMEM((64, 128), BF16),
            pltpu.VMEM((1, 64), jnp.int32),
            pltpu.VMEM((1, 64), jnp.int32),
            pltpu.SemaphoreType.DMA((4,)),
            pltpu.SemaphoreType.DMA((5,)),
        ],
        compiler_params=PARAMS,
        cost_estimate=cost(2048 * 2048, 1 << 21),
    )(
        in_hbm(pair),
        in_hbm(bias_gain[None]),
        in_hbm(w_pair_bias.T),
        in_hbm(atoms),
        in_hbm(atom_token[None]),
        in_hbm(atom_mask[None]),
    )


def atom_block(band, cross, pack, gain, w_qkvg, w_out, mid_gain, w_rest, after):
    return pl.pallas_call(
        atom_kernel,
        in_specs=whole(15) + [ANY],
        out_specs=whole(2),
        out_shape=[
            jax.ShapeDtypeStruct((ATOMS, 128), BF16),
            jax.ShapeDtypeStruct((128, 128), BF16),
        ],
        compiler_params=PARAMS,
        cost_estimate=cost(1 << 25, 1 << 20),
    )(band, cross, pack, gain[None], *w_qkvg, w_out, mid_gain[None], *w_rest, after)


def spread_terms(along, after):
    return pl.pallas_call(
        spread_kernel,
        in_specs=whole(1) + [ANY],
        out_specs=whole(1)[0],
        out_shape=jax.ShapeDtypeStruct((512, 128), BF16),
        compiler_params=PARAMS,
    )(along, after)


def add_terms(held, came):
    return pl.pallas_call(
        add_kernel,
        in_specs=whole(2),
        out_specs=HBM,
        out_shape=jax.ShapeDtypeStruct(held.shape, BF16),
        scratch_shapes=[
            pltpu.VMEM(held.shape, BF16),
            pltpu.SemaphoreType.DMA((held.shape[0] // PAIR_ROWS,)),
        ],
        compiler_params=PARAMS,
    )(held, came)


def body(
    pair, atoms, atom_token, atom_mask, bias_gain, w_pair_bias, trans_gain, w_pair_up, w_pair_down,
    atom_gain, w_query, w_key, w_value, w_gate, w_out, mid_gain, w_atom_up, w_atom_down, w_single,
    w_outer_row, w_outer_col,
):
    joint = ("row", "col")
    band, pack = near_diagonal(pair, bias_gain, w_pair_bias, atoms, atom_token, atom_mask)
    band = lax.all_to_all(band, joint, 0, 0, tiled=True, axis_index_groups=ROW_GROUPS)
    ends = [(16 * i + 15, 16 * i + 16) for i in range(31)]
    cross = lax.ppermute(pack, joint, ends + [(j, i) for i, j in ends])
    trans = (trans_gain[None], w_pair_up, w_pair_down)
    held = transition(pair, *trans, 0, pack)
    w_qkvg = (w_query, w_key, w_value, w_gate)
    w_rest = (w_atom_up, w_atom_down, w_single, w_outer_row, w_outer_col)
    atoms_out, terms = atom_block(
        band, cross, pack, atom_gain, w_qkvg, w_out, mid_gain, w_rest, held
    )
    along = lax.all_to_all(terms, joint, 0, 0, tiled=True, axis_index_groups=Z_GROUPS)
    held = transition(held, *trans, 1, terms)
    going = spread_terms(along, held)
    came = lax.all_to_all(going, joint, 0, 0, tiled=True, axis_index_groups=PLANE_GROUPS)
    held = transition(held, *trans, 2, going)
    came, held = lax.optimization_barrier((came, held))
    came = lax.all_gather(came, "row", axis=0, tiled=True, axis_index_groups=CORE_GROUPS)
    return (atoms_out, add_terms(held, came))


def solution(mesh):
    spread = P(("row", "col"))
    in_specs = (P("row", "col", None), P(("row", "col"), None), spread, spread) + (P(),) * 17
    out_specs = (P(("row", "col"), None), P("row", "col", None))
    return jax.shard_map(body, mesh=mesh, in_specs=in_specs, out_specs=out_specs, check_vma=False)
```
